32 devices in a mesh: row: 8 (over z, x), col: 4 (over y, core).
Axes of the slice: x: 2, y: 2, z: 4, core: 2. Of those that a mesh axis runs over, the one named last changes fastest.
Arguments:
- front: float32 [12, 1024, 24, 512], P(None, 'row', None, 'col')
- children: float32 [32768, 8192], P('row', 'col')
- block_map: int32 [4, 64], replicated, may hold values from -1 to 95, as said below
- child_at: int32 [4], replicated, may hold values from 0 to 3, each once
Outputs:
- factored: float32 [12, 1024, 24, 512], P(None, 'row', None, 'col')
The draws below stay inside these ranges and needn't reach their ends.
Inputs may be any that keep to these rules, and one draw needn't show every extreme that they name: Entry block_map[k, t * 8 + p] is -1 or a parent block b with b % 8 == p. For each child k and each p the entries that are not -1 come first in t, increase, and number 8 // 2 to 8; for every child both of these counts occur. No block appears twice for one child. `child_at`: each child stands in exactly one slot.
All inputs are finite; a program needn't handle non-finite values.
Results may differ from the reference program's by a relative error of at most 0.00005.
Values sent between devices are 32-bit elements; how exact they have to be, the bound alone decides.
No kernel may reach another device: no remote copies, remote signals or barrier semaphores. Data moves between devices by JAX's collectives and lax.ppermute only.
A program may use at most 256 MiB of HBM per device.

```python
import math
import jax
import jax.numpy as jnp
from jax import lax

BS = 128
NBLK = 96
CHILD = 4
PB = 8
LBR = 12
LBC = 24
CAPR = 8
RSLOTS = 64
CSLOTS = 64
ROW_SPAN = 1024
COL_SPAN = 512


def draw_front(key, part):
    array_shape = (LBR, ROW_SPAN, LBC, COL_SPAN)
    noise_key = jax.random.fold_in(key, 11)
    boost_key = jax.random.fold_in(key, 12)
    noise_part = jnp.clip(jax.random.normal(noise_key, array_shape, jnp.float32), -6.0, 6.0)
    diag_boost = jax.random.uniform(boost_key, array_shape, jnp.float32, 8.0, 16.0) * math.sqrt(PB * BS)
    row_ids = jnp.arange(LBR)[:, None, None, None] * ROW_SPAN + jnp.arange(ROW_SPAN)[None, :, None, None]
    col_ids = jnp.arange(LBC)[None, None, :, None] * COL_SPAN + jnp.arange(COL_SPAN)[None, None, None, :]
    return noise_part + jnp.where(row_ids == col_ids, diag_boost, 0.0)


def draw_children(key, part):
    array_shape = (CHILD * RSLOTS * BS, CSLOTS * BS)
    value_key = jax.random.fold_in(key, 22)
    return jnp.clip(jax.random.normal(value_key, array_shape, jnp.float32), -6.0, 6.0)


def draw_block_map(key, part):
    groups = RSLOTS // CAPR
    counts = jax.random.randint(jax.random.fold_in(key, 31), (CHILD, groups), CAPR // 2, CAPR + 1)
    low_owner = jax.random.randint(jax.random.fold_in(key, 32), (CHILD,), 0, groups)
    high_owner = (low_owner + 1 + jax.random.randint(jax.random.fold_in(key, 33), (CHILD,), 0, groups - 1)) % groups
    owner_ids = jnp.arange(groups)[None, :]
    counts = jnp.where(owner_ids == low_owner[:, None], CAPR // 2, counts)
    counts = jnp.where(owner_ids == high_owner[:, None], CAPR, counts)
    subkeys = jax.random.split(jax.random.fold_in(key, 34), CHILD * groups)
    permuted = jax.vmap(lambda subkey: jax.random.permutation(subkey, LBR))(subkeys)
    permuted = permuted.reshape(CHILD, groups, LBR)[:, :, :CAPR]
    slot_ids = jnp.arange(CAPR)[None, None, :]
    chosen = jnp.sort(jnp.where(slot_ids < counts[:, :, None], permuted, LBR), axis=2)
    mapped = jnp.where(chosen < LBR, chosen * groups + owner_ids[:, :, None], -1)
    return mapped.transpose(0, 2, 1).reshape(CHILD, CAPR * groups).astype(jnp.int32)


def setup_inputs(seed: int = 0) -> dict:
    key_of = jax.random.split(jax.random.key(seed), 5)
    return {
        "front": draw_front(jax.random.fold_in(key_of[4], 71), 0),
        "children": draw_children(jax.random.fold_in(key_of[4], 71), 0),
        "block_map": draw_block_map(jax.random.fold_in(key_of[4], 71), 0),
        "child_at": jax.random.permutation(key_of[3], CHILD).astype(jnp.int32),
    }


def reference(front, children, block_map, child_at):
    grid_rows = ROW_SPAN // BS
    grid_cols = COL_SPAN // BS
    fanout = grid_rows // grid_cols
    front_order = NBLK * BS
    panel_width = PB * BS
    blocks = front.reshape(NBLK, BS, NBLK, BS)
    pieces = children.reshape(CHILD, RSLOTS, BS, CSLOTS, BS)
    for slot_index in range(CHILD):
        mapping = block_map[child_at[slot_index]]
        columns = mapping.reshape(CAPR, fanout, grid_cols).transpose(2, 1, 0).reshape(CSLOTS)
        rows_to = jnp.where(mapping >= 0, mapping, NBLK).astype(jnp.int32)
        cols_to = jnp.where(columns >= 0, columns, NBLK).astype(jnp.int32)
        blocks = blocks.at[rows_to[:, None], :, cols_to[None, :], :].add(pieces[slot_index].transpose(0, 2, 1, 3), mode='drop')
    whole = blocks.reshape(front_order, front_order)
    corner = whole[:panel_width, :panel_width]
    factor = jnp.tril(jnp.linalg.cholesky(0.5 * (corner + corner.T)))
    lower_part = jax.scipy.linalg.solve_triangular(factor, whole[panel_width:, :panel_width].T, lower=True).T
    trailing = whole[panel_width:, panel_width:] - jnp.dot(lower_part, lower_part.T, precision=lax.Precision.HIGHEST)
    result = whole.at[:panel_width, :panel_width].set(factor)
    result = result.at[panel_width:, :panel_width].set(lower_part)
    result = result.at[panel_width:, panel_width:].set(trailing)
    return result.reshape(LBR, ROW_SPAN, LBC, COL_SPAN)
```

```python
import jax
import jax.numpy as jnp
from jax import lax
from jax.experimental import pallas as pl
from jax.experimental.pallas import tpu as pltpu
from jax.sharding import PartitionSpec as P

CHILD = 4
PB = 8
HIGHEST_PRECISION = lax.Precision.HIGHEST
VMEM_LIMIT = 56 * 1024 * 1024


def split_halves(value):
    rounded = lax.reduce_precision(value, exponent_bits=8, mantissa_bits=7)
    return rounded.astype(jnp.bfloat16), (value - rounded).astype(jnp.bfloat16)


def add_slot(out_ref, source_ref, row_count, tile_cols, block, lane_start, block_size):
    for start in range(0, row_count, 8):
        place = pl.ds(start * tile_cols + block, 8, stride=tile_cols)
        out_ref[0, place, :] += source_ref[0, start : start + 8, lane_start : lane_start + block_size]


def base_kernel(
    rows_ref, cols_ref, place_ref, front_ref, own_high, own_low, across_high, across_low, *rest,
    tile_cols, block_size, panel_tiles,
):
    head_refs = rest[:panel_tiles]
    slot_refs = rest[panel_tiles:-1]
    out_ref = rest[-1]
    row_count = own_high.shape[0]
    tile = pl.program_id(0)
    group = 2 if tile_cols % 2 == 0 else 1
    width = group * block_size
    for first in range(0, tile_cols, group):
        lanes = slice(first * block_size, first * block_size + width)
        dims = (((1,), (1,)), ((), ()))
        product = lax.dot_general(
            own_high[...], across_high[lanes, :], dims, preferred_element_type=jnp.float32
        )
        product += lax.dot_general(
            own_high[...], across_low[lanes, :], dims, preferred_element_type=jnp.float32
        )
        product += lax.dot_general(
            own_low[...], across_high[lanes, :], dims, preferred_element_type=jnp.float32
        )
        for offset in range(group):
            block = first + offset
            for start in range(0, row_count, 8):
                place = pl.ds(start * tile_cols + block, 8, stride=tile_cols)
                if block < panel_tiles:
                    out_ref[0, place, :] = head_refs[block][start : start + 8, :]
                else:
                    piece = product[start : start + 8, offset * block_size : (offset + 1) * block_size]
                    out_ref[0, place, :] = front_ref[0, place, :] - piece
    for child in range(CHILD):
        for slot in range(panel_tiles):
            block = cols_ref[child, slot]

            @pl.when((rows_ref[child, tile] >= 0) & (block >= 0))
            def _():
                add_slot(
                    out_ref, slot_refs[child], row_count, tile_cols, block, slot * block_size, block_size
                )


def add_kernel(rows_ref, cols_ref, base_ref, *rest, tile_cols, block_size, slot_count):
    slot_refs = rest[:-1]
    out_ref = rest[-1]
    row_count = slot_refs[0].shape[1]
    tile = pl.program_id(0)
    out_ref[...] = base_ref[...]
    for child in range(CHILD):

        @pl.when(rows_ref[child, tile] >= 0)
        def _():
            for slot in range(slot_count):
                block = cols_ref[child, slot]

                @pl.when(block >= 0)
                def _():
                    add_slot(
                        out_ref, slot_refs[child], row_count, tile_cols, block, slot * block_size, block_size
                    )


def slot_spec(child, rows, width):
    def index(tile, part, rows_ref, *_):
        source = rows_ref[child, tile]
        there = source >= 0
        return jnp.where(there, source, 0), jnp.where(there, part, 0), 0

    return pl.BlockSpec((1, rows, width), index)


def make_base(front, own, across, heads, slots, row_table, col_table, place, panel_tiles, tile_cols):
    tile_rows = front.shape[0]
    block_size = front.shape[2]
    rows = block_size
    depth = own[0].shape[1]
    flat = pl.BlockSpec((1, rows * tile_cols, block_size), lambda a, x, *_: (a, x, 0))
    own_spec = pl.BlockSpec((rows, depth), lambda a, x, *_: (a, 0))
    whole_spec = pl.BlockSpec(across[0].shape, lambda a, x, *_: (0, 0), pipeline_mode=pl.Buffered(1))
    grid_cols = depth // block_size // panel_tiles

    def head_spec(tile):
        return pl.BlockSpec(
            (rows, block_size), lambda a, x, r, c, place_ref: (a, tile * grid_cols + place_ref[0])
        )

    return pl.pallas_call(
        lambda *refs: base_kernel(
            *refs, tile_cols=tile_cols, block_size=block_size, panel_tiles=panel_tiles
        ),
        grid_spec=pltpu.PrefetchScalarGridSpec(
            num_scalar_prefetch=3,
            grid=(tile_rows, 1),
            in_specs=[flat, own_spec, own_spec, whole_spec, whole_spec]
            + [head_spec(tile) for tile in range(panel_tiles)]
            + [slot_spec(child, rows, panel_tiles * block_size) for child in range(CHILD)],
            out_specs=flat,
        ),
        out_shape=jax.ShapeDtypeStruct(front.shape, jnp.float32),
        compiler_params=pltpu.CompilerParams(vmem_limit_bytes=VMEM_LIMIT),
        cost_estimate=pl.CostEstimate(
            flops=6 * tile_rows * rows * depth * across[0].shape[0],
            bytes_accessed=60_000_000,
            transcendentals=0,
        ),
        name="trailing_base",
    )(
        row_table, col_table, place, front, own[0], own[1], across[0], across[1],
        *([heads] * panel_tiles), *([slots] * CHILD),
    )


def make_final(base, slots, row_table, col_table, tile_cols):
    tile_rows = base.shape[0]
    block_size = base.shape[2]
    rows = block_size // 2
    width = slots.shape[2]
    flat = pl.BlockSpec((1, rows * tile_cols, block_size), lambda a, x, *_: (a, x, 0))
    return pl.pallas_call(
        lambda *refs: add_kernel(
            *refs, tile_cols=tile_cols, block_size=block_size, slot_count=width // block_size
        ),
        grid_spec=pltpu.PrefetchScalarGridSpec(
            num_scalar_prefetch=2,
            grid=(tile_rows, block_size // rows),
            in_specs=[flat] + [slot_spec(child, rows, width) for child in range(CHILD)],
            out_specs=flat,
        ),
        out_shape=jax.ShapeDtypeStruct(base.shape, jnp.float32),
        compiler_params=pltpu.CompilerParams(vmem_limit_bytes=VMEM_LIMIT),
        cost_estimate=pl.CostEstimate(flops=0, bytes_accessed=70_000_000, transcendentals=0),
        name="extend_add",
    )(row_table, col_table, base, *([slots] * CHILD))


def body(front, children, block_map, child_at):
    grid_rows = lax.axis_size("row")
    grid_cols = lax.axis_size("col")
    row_index = lax.axis_index("row")
    col_index = lax.axis_index("col")
    tile_rows, block_size, tile_cols, _ = front.shape
    slot_cap = block_map.shape[1] // grid_rows
    fanout = grid_rows // grid_cols
    group_cap = slot_cap * fanout
    per_device = CHILD * slot_cap // grid_rows
    slot_rows = CHILD * slot_cap
    panel_width = PB * block_size
    panel_tiles = (PB + grid_cols - 1) // grid_cols
    diag_tiles = (PB + grid_rows - 1) // grid_rows
    local_rows = tile_rows * block_size
    piece_width = panel_tiles * block_size

    slot_maps = jnp.take(block_map, child_at, axis=0)
    own_maps = jnp.take(slot_maps.reshape(CHILD, slot_cap, grid_rows), row_index, axis=2)
    row_hit = (own_maps[:, :, None] >= 0) & (
        own_maps[:, :, None] // grid_rows == jnp.arange(tile_rows)[None, None, :]
    )
    slot_ids = jnp.arange(slot_rows, dtype=jnp.int32).reshape(CHILD, slot_cap)
    row_table = jnp.max(jnp.where(row_hit, slot_ids[:, :, None], -1), axis=1).astype(jnp.int32)
    columns = jnp.take(slot_maps.reshape(CHILD, slot_cap, fanout, grid_cols), col_index, axis=3)
    columns = columns.transpose(0, 2, 1)
    column_blocks = jnp.where(columns >= 0, columns // grid_cols, -1).astype(jnp.int32)
    in_panel = (columns[:, :panel_tiles, 0] >= 0) & (columns[:, :panel_tiles, 0] < PB)
    early_table = jnp.where(in_panel, -1, column_blocks[:, :panel_tiles, 0])
    late_table = jnp.concatenate(
        [column_blocks[:, j, (1 if j < panel_tiles else 0) :] for j in range(fanout)], axis=1
    )
    place = col_index.astype(jnp.int32).reshape(1)

    def to_rows(parts):
        packed = jnp.concatenate(parts, axis=1)
        packed = packed.reshape(per_device, grid_rows, block_size, packed.shape[1])
        return packed.transpose(1, 0, 2, 3)

    def exchange(packed):
        got = lax.all_to_all(packed, "row", split_axis=0, concat_axis=0, tiled=True)
        return got.reshape(slot_rows, block_size, packed.shape[3])

    span = slot_cap * block_size
    early = exchange(
        to_rows([children[:, j * span : j * span + block_size] for j in range(panel_tiles)])
    )
    late_send = to_rows(
        [
            children[:, j * span + (block_size if j < panel_tiles else 0) : (j + 1) * span]
            for j in range(fanout)
        ]
    )
    lane_mask = jnp.repeat(in_panel, block_size, axis=1).astype(jnp.float32)
    masked = early.reshape(CHILD, slot_cap, block_size, piece_width) * lane_mask[:, None, None, :]
    piece = jnp.einsum(
        "cta,ctxw->axw", row_hit.astype(jnp.float32), masked, precision=HIGHEST_PRECISION
    )
    piece = piece + front[:, :, :panel_tiles].reshape(tile_rows, block_size, piece_width)

    piece = piece.reshape(local_rows, piece_width)
    turn = [
        (g * grid_cols + q, ((g // grid_cols) * grid_cols + q) * grid_cols + g % grid_cols)
        for g in range(grid_rows)
        for q in range(grid_cols)
    ]
    turned = lax.ppermute(piece, ("row", "col"), turn)
    across_panel = lax.all_gather(turned, "row", axis=0, tiled=False)
    piece, across_panel, late_send = lax.optimization_barrier((piece, across_panel, late_send))
    late = exchange(late_send)

    top = across_panel.reshape(fanout, grid_cols, local_rows, piece_width)[
        :, :, : diag_tiles * block_size
    ]
    corner = lax.all_gather(top, "col", axis=0, tiled=False)
    corner = corner.reshape(
        grid_cols, fanout, grid_cols, diag_tiles, block_size, panel_tiles, block_size
    )
    corner = corner.transpose(3, 1, 0, 4, 5, 2, 6).reshape(
        diag_tiles * grid_rows * block_size, panel_width
    )[:panel_width]
    own_panel = lax.all_gather(piece, "col", axis=0, tiled=False)
    across_panel = across_panel.reshape(fanout, grid_cols, local_rows, piece_width)

    factor = jnp.linalg.cholesky(0.5 * (corner + corner.T))
    inverse = jax.scipy.linalg.solve_triangular(
        factor, jnp.eye(panel_width, dtype=jnp.float32), lower=True
    )
    weights = inverse.reshape(panel_width, panel_tiles, grid_cols, block_size)
    weights = weights.transpose(2, 1, 3, 0).reshape(grid_cols, piece_width, panel_width)

    own = jnp.einsum("crw,cwn->rn", own_panel, weights, precision=HIGHEST_PRECISION)
    across = jnp.einsum("fcrw,cwn->frn", across_panel, weights, precision=HIGHEST_PRECISION)

    own = own.reshape(tile_rows, block_size, panel_width)
    own_blocks = jnp.arange(tile_rows) * grid_rows + row_index
    own_below = (own_blocks >= PB)[:, None, None]
    top = lax.dynamic_slice_in_dim(
        factor, jnp.minimum(row_index, PB - 1) * block_size, block_size, axis=0
    )
    heads = jnp.where(own_below, own, top[None]).reshape(local_rows, panel_width)
    own_halves = split_halves(jnp.where(own_below, own, 0.0).reshape(local_rows, panel_width))
    across = across.reshape(fanout, tile_rows, block_size, panel_width).transpose(1, 0, 2, 3)
    across_blocks = jnp.arange(tile_cols) * grid_cols + col_index
    across = jnp.where(
        (across_blocks >= PB)[:, None, None],
        across.reshape(tile_cols, block_size, panel_width),
        0.0,
    )
    across_halves = split_halves(across.reshape(tile_cols * block_size, panel_width))

    flat = front.reshape(tile_rows, block_size * tile_cols, block_size)
    base = make_base(
        flat, own_halves, across_halves, heads, early, row_table, early_table, place,
        panel_tiles, tile_cols,
    )
    result = make_final(base, late, row_table, late_table, tile_cols)
    return result.reshape(front.shape)


def solution(mesh):
    in_specs = (P(None, "row", None, "col"), P("row", "col"), P(), P())
    out_specs = P(None, "row", None, "col")
    return jax.shard_map(body, mesh=mesh, in_specs=in_specs, out_specs=out_specs, check_vma=False)
```

```python
import jax
import jax.numpy as jnp
from jax import lax
from jax.experimental import pallas as pl
from jax.experimental.pallas import tpu as pltpu
from jax.sharding import PartitionSpec as P

CHILD = 4
PB = 8
HIGHEST_PRECISION = lax.Precision.HIGHEST
VMEM_LIMIT = 56 * 1024 * 1024


def split_halves(value):
    rounded = lax.reduce_precision(value, exponent_bits=8, mantissa_bits=7)
    return rounded.astype(jnp.bfloat16), (value - rounded).astype(jnp.bfloat16)


def add_slot(out_ref, source_ref, row_count, tile_cols, block, lane_start, block_size):
    for start in range(0, row_count, 8):
        place = pl.ds(start * tile_cols + block, 8, stride=tile_cols)
        out_ref[0, place, :] += source_ref[0, start : start + 8, lane_start : lane_start + block_size]


def base_kernel(
    rows_ref, cols_ref, place_ref, front_ref, own_high, own_low, across_high, across_low, *rest,
    tile_cols, block_size, panel_tiles,
):
    head_refs = rest[:panel_tiles]
    slot_refs = rest[panel_tiles:-1]
    out_ref = rest[-1]
    row_count = own_high.shape[0]
    tile = pl.program_id(0)
    group = 2 if tile_cols % 2 == 0 else 1
    width = group * block_size
    for first in range(0, tile_cols, group):
        lanes = slice(first * block_size, first * block_size + width)
        dims = (((1,), (1,)), ((), ()))
        product = lax.dot_general(
            own_high[...], across_high[lanes, :], dims, preferred_element_type=jnp.float32
        )
        product += lax.dot_general(
            own_high[...], across_low[lanes, :], dims, preferred_element_type=jnp.float32
        )
        product += lax.dot_general(
            own_low[...], across_high[lanes, :], dims, preferred_element_type=jnp.float32
        )
        for offset in range(group):
            block = first + offset
            for start in range(0, row_count, 8):
                place = pl.ds(start * tile_cols + block, 8, stride=tile_cols)
                if block < panel_tiles:
                    out_ref[0, place, :] = head_refs[block][start : start + 8, :]
                else:
                    piece = product[start : start + 8, offset * block_size : (offset + 1) * block_size]
                    out_ref[0, place, :] = front_ref[0, place, :] - piece
    for child in range(CHILD):
        for slot in range(panel_tiles):
            block = cols_ref[child, slot]

            @pl.when((rows_ref[child, tile] >= 0) & (block >= 0))
            def _():
                add_slot(
                    out_ref, slot_refs[child], row_count, tile_cols, block, slot * block_size, block_size
                )


def add_kernel(rows_ref, cols_ref, base_ref, *rest, tile_cols, block_size, slot_count):
    slot_refs = rest[:-1]
    out_ref = rest[-1]
    row_count = slot_refs[0].shape[1]
    tile = pl.program_id(0)
    out_ref[...] = base_ref[...]
    for child in range(CHILD):

        @pl.when(rows_ref[child, tile] >= 0)
        def _():
            for slot in range(slot_count):
                block = cols_ref[child, slot]

                @pl.when(block >= 0)
                def _():
                    add_slot(
                        out_ref, slot_refs[child], row_count, tile_cols, block, slot * block_size, block_size
                    )


def slot_spec(child, rows, width):
    def index(tile, part, rows_ref, *_):
        source = rows_ref[child, tile]
        there = source >= 0
        return jnp.where(there, source, 0), jnp.where(there, part, 0), 0

    return pl.BlockSpec((1, rows, width), index)


def make_base(front, own, across, heads, slots, row_table, col_table, place, panel_tiles, tile_cols):
    tile_rows = front.shape[0]
    block_size = front.shape[2]
    rows = block_size
    depth = own[0].shape[1]
    flat = pl.BlockSpec((1, rows * tile_cols, block_size), lambda a, x, *_: (a, x, 0))
    own_spec = pl.BlockSpec((rows, depth), lambda a, x, *_: (a, 0))
    whole_spec = pl.BlockSpec(across[0].shape, lambda a, x, *_: (0, 0), pipeline_mode=pl.Buffered(1))
    grid_cols = depth // block_size // panel_tiles

    def head_spec(tile):
        return pl.BlockSpec(
            (rows, block_size), lambda a, x, r, c, place_ref: (a, tile * grid_cols + place_ref[0])
        )

    return pl.pallas_call(
        lambda *refs: base_kernel(
            *refs, tile_cols=tile_cols, block_size=block_size, panel_tiles=panel_tiles
        ),
        grid_spec=pltpu.PrefetchScalarGridSpec(
            num_scalar_prefetch=3,
            grid=(tile_rows, 1),
            in_specs=[flat, own_spec, own_spec, whole_spec, whole_spec]
            + [head_spec(tile) for tile in range(panel_tiles)]
            + [slot_spec(child, rows, panel_tiles * block_size) for child in range(CHILD)],
            out_specs=flat,
        ),
        out_shape=jax.ShapeDtypeStruct(front.shape, jnp.float32),
        compiler_params=pltpu.CompilerParams(vmem_limit_bytes=VMEM_LIMIT),
        cost_estimate=pl.CostEstimate(
            flops=6 * tile_rows * rows * depth * across[0].shape[0],
            bytes_accessed=60_000_000,
            transcendentals=0,
        ),
        name="trailing_base",
    )(
        row_table, col_table, place, front, own[0], own[1], across[0], across[1],
        *([heads] * panel_tiles), *([slots] * CHILD),
    )


def across_kernel(in_top_ref, *rest, count, diag_tiles):
    piece_refs = rest[:count]
    weight_high, weight_low, high_ref, low_ref = rest[count:]
    tiles, _, block_size, depth = high_ref.shape
    rows = tiles * block_size
    total = jnp.zeros((rows, depth), jnp.float32)
    for index in range(count):
        value = piece_refs[index][...].reshape(rows, weight_high.shape[1])
        high = value.astype(jnp.bfloat16)
        low = (value - high.astype(jnp.float32)).astype(jnp.bfloat16)
        for left, right in ((high, weight_high), (high, weight_low), (low, weight_high)):
            total += jnp.dot(left, right[index], preferred_element_type=jnp.float32)
    first_tile = pl.program_id(1) * tiles
    row_ids = lax.broadcasted_iota(jnp.int32, (rows, depth), 0)
    corner_rows = jnp.where(
        in_top_ref[pl.program_id(0)] > 0, (diag_tiles - first_tile) * block_size, 0
    )
    total = jnp.where(row_ids < corner_rows, 0.0, total)
    high = total.astype(jnp.bfloat16)
    high_ref[...] = high.reshape(high_ref.shape)
    low_ref[...] = (total - high.astype(jnp.float32)).astype(jnp.bfloat16).reshape(low_ref.shape)


def make_across(pieces, weights, in_top, tile_rows, diag_tiles):
    count, fanout, local_rows, width = pieces.shape
    block_size = local_rows // tile_rows
    depth = weights[0].shape[2]
    tiles = next(n for n in (4, 3, 2, 1) if tile_rows % n == 0)

    def piece_spec(index):
        return pl.BlockSpec(
            (1, 1, tiles * block_size, width), lambda f, a, *_: (index, f, a, 0)
        )

    weight_spec = pl.BlockSpec(
        weights[0].shape, lambda f, a, *_: (0, 0, 0), pipeline_mode=pl.Buffered(1)
    )
    out_spec = pl.BlockSpec((tiles, 1, block_size, depth), lambda f, a, *_: (a, f, 0, 0))
    out_shape = jax.ShapeDtypeStruct((tile_rows, fanout, block_size, depth), jnp.bfloat16)
    outs = pl.pallas_call(
        lambda *refs: across_kernel(*refs, count=count, diag_tiles=diag_tiles),
        grid_spec=pltpu.PrefetchScalarGridSpec(
            num_scalar_prefetch=1,
            grid=(fanout, tile_rows // tiles),
            in_specs=[piece_spec(index) for index in range(count)] + [weight_spec] * 2,
            out_specs=[out_spec] * 2,
        ),
        out_shape=[out_shape] * 2,
        compiler_params=pltpu.CompilerParams(vmem_limit_bytes=VMEM_LIMIT),
        cost_estimate=pl.CostEstimate(
            flops=6 * fanout * local_rows * depth * depth,
            bytes_accessed=30_000_000,
            transcendentals=0,
        ),
        name="across_rows",
    )(in_top, *([pieces] * count), *weights)
    return [out.reshape(tile_rows * fanout * block_size, depth) for out in outs]


def make_final(base, slots, row_table, col_table, tile_cols):
    tile_rows = base.shape[0]
    block_size = base.shape[2]
    rows = block_size // 2
    width = slots.shape[2]
    flat = pl.BlockSpec((1, rows * tile_cols, block_size), lambda a, x, *_: (a, x, 0))
    return pl.pallas_call(
        lambda *refs: add_kernel(
            *refs, tile_cols=tile_cols, block_size=block_size, slot_count=width // block_size
        ),
        grid_spec=pltpu.PrefetchScalarGridSpec(
            num_scalar_prefetch=2,
            grid=(tile_rows, block_size // rows),
            in_specs=[flat] + [slot_spec(child, rows, width) for child in range(CHILD)],
            out_specs=flat,
        ),
        out_shape=jax.ShapeDtypeStruct(base.shape, jnp.float32),
        compiler_params=pltpu.CompilerParams(vmem_limit_bytes=VMEM_LIMIT),
        cost_estimate=pl.CostEstimate(flops=0, bytes_accessed=70_000_000, transcendentals=0),
        name="extend_add",
    )(row_table, col_table, base, *([slots] * CHILD))


def factor_and_inverse(matrix, block_size):
    size = matrix.shape[0]
    blocks = size // block_size
    eye = jnp.eye(block_size, dtype=jnp.float32)

    def multiply(left, right):
        return jnp.dot(left, right, precision=HIGHEST_PRECISION)

    columns, inverses = [], []
    trailing = matrix
    for k in range(blocks):
        head = lax.linalg.cholesky(trailing[:block_size, :block_size], symmetrize_input=False)
        inverses.append(lax.linalg.triangular_solve(head, eye, left_side=True, lower=True))
        below = multiply(trailing[block_size:, :block_size], inverses[k].T)
        trailing = trailing[block_size:, block_size:] - multiply(below, below.T)
        above = jnp.zeros((k * block_size, block_size), jnp.float32)
        columns.append(jnp.concatenate([above, head, below], axis=0))
    factor = jnp.concatenate(columns, axis=1)
    inverse = jnp.zeros((0, size), jnp.float32)
    for k in range(blocks):
        start, stop = k * block_size, (k + 1) * block_size
        row = jnp.pad(inverses[k], ((0, 0), (start, size - stop)))
        if k:
            row -= multiply(inverses[k], multiply(factor[start:stop, :start], inverse))
        inverse = jnp.concatenate([inverse, row], axis=0)
    return factor, inverse


def body(front, children, block_map, child_at):
    grid_rows = lax.axis_size("row")
    grid_cols = lax.axis_size("col")
    row_index = lax.axis_index("row")
    col_index = lax.axis_index("col")
    tile_rows, block_size, tile_cols, _ = front.shape
    slot_cap = block_map.shape[1] // grid_rows
    fanout = grid_rows // grid_cols
    group_cap = slot_cap * fanout
    per_device = CHILD * slot_cap // grid_rows
    slot_rows = CHILD * slot_cap
    panel_width = PB * block_size
    panel_tiles = (PB + grid_cols - 1) // grid_cols
    diag_tiles = (PB + grid_rows - 1) // grid_rows
    local_rows = tile_rows * block_size
    piece_width = panel_tiles * block_size

    slot_maps = jnp.take(block_map, child_at, axis=0)
    own_maps = jnp.take(slot_maps.reshape(CHILD, slot_cap, grid_rows), row_index, axis=2)
    row_hit = (own_maps[:, :, None] >= 0) & (
        own_maps[:, :, None] // grid_rows == jnp.arange(tile_rows)[None, None, :]
    )
    slot_ids = jnp.arange(slot_rows, dtype=jnp.int32).reshape(CHILD, slot_cap)
    row_table = jnp.max(jnp.where(row_hit, slot_ids[:, :, None], -1), axis=1).astype(jnp.int32)
    columns = jnp.take(slot_maps.reshape(CHILD, slot_cap, fanout, grid_cols), col_index, axis=3)
    columns = columns.transpose(0, 2, 1)
    column_blocks = jnp.where(columns >= 0, columns // grid_cols, -1).astype(jnp.int32)
    in_panel = (columns[:, :panel_tiles, 0] >= 0) & (columns[:, :panel_tiles, 0] < PB)
    early_table = jnp.where(in_panel, -1, column_blocks[:, :panel_tiles, 0])
    late_table = jnp.concatenate(
        [column_blocks[:, j, (1 if j < panel_tiles else 0) :] for j in range(fanout)], axis=1
    )
    place = col_index.astype(jnp.int32).reshape(1)

    def to_rows(packed):
        packed = packed.reshape(per_device, grid_rows, block_size, packed.shape[1])
        return packed.transpose(1, 0, 2, 3)

    def exchange(packed):
        return lax.all_to_all(packed, "row", split_axis=0, concat_axis=0, tiled=True)

    span = slot_cap * block_size
    early_send = to_rows(
        jnp.concatenate(
            [children[:, j * span : j * span + block_size] for j in range(panel_tiles)], axis=1
        )
    )

    late_send = to_rows(
        jnp.concatenate(
            [
                children[:, j * span + (block_size if j < panel_tiles else 0) : (j + 1) * span]
                for j in range(fanout)
            ],
            axis=1,
        )
    )
    lane_mask = jnp.repeat(in_panel, block_size, axis=1).astype(jnp.float32)

    first = exchange(early_send[:, :1])
    corner_slots = first[:: slot_cap // per_device, 0]
    corner_hit = row_hit[:, 0, :diag_tiles].astype(jnp.float32)
    corner_piece = jnp.sum(
        corner_hit[:, :, None, None] * (corner_slots * lane_mask[:, None, :])[:, None], axis=0
    )
    front_piece = front[:, :, :panel_tiles].reshape(tile_rows, block_size, piece_width)
    corner_piece = corner_piece + front_piece[:diag_tiles]
    rest_send = early_send[:, 1:]
    if per_device > 1:
        first, rest_send = lax.optimization_barrier((first, rest_send))
        early = jnp.concatenate([first, exchange(rest_send)], axis=1)
    else:
        early = first
    early = early.reshape(slot_rows, block_size, piece_width)

    corner_pieces = lax.all_gather(corner_piece, ("row", "col"), axis=0, tiled=False)
    masked = early.reshape(CHILD, slot_cap, block_size, piece_width) * lane_mask[:, None, None, :]
    piece = jnp.einsum(
        "cta,ctxw->axw", row_hit.astype(jnp.float32), masked, precision=HIGHEST_PRECISION
    )
    piece = (piece + front_piece).reshape(local_rows, piece_width)

    piece, corner_pieces = lax.optimization_barrier((piece, corner_pieces))

    corner = corner_pieces.reshape(grid_rows, grid_cols, diag_tiles, block_size, panel_tiles, block_size)
    corner = corner.transpose(2, 0, 3, 4, 1, 5).reshape(
        diag_tiles * grid_rows * block_size, panel_width
    )[:panel_width]

    def turned(shift):
        pairs = []
        for g in range(grid_rows):
            part = (g // grid_cols + shift) % fanout
            for q in range(grid_cols):
                pairs.append((g * grid_cols + q, (part * grid_cols + q) * grid_cols + g % grid_cols))
        return lax.ppermute(piece, ("row", "col"), pairs)

    by_shift = [turned(shift) for shift in range(fanout)]
    part_index = row_index // grid_cols
    turned_pieces = []
    for f in range(fanout):
        chosen = by_shift[0]
        for shift in range(1, fanout):
            chosen = jnp.where((part_index - shift) % fanout == f, by_shift[shift], chosen)
        turned_pieces.append(chosen)
    turned_pieces = jnp.stack(turned_pieces)

    turned_pieces, piece, late_send = lax.optimization_barrier((turned_pieces, piece, late_send))
    late = exchange(late_send).reshape(slot_rows, block_size, late_send.shape[3])
    own_panel = lax.all_gather(piece, "col", axis=0, tiled=False)
    turned_pieces, own_panel = lax.optimization_barrier((turned_pieces, own_panel))
    parts = [[h * grid_cols + q for q in range(grid_cols)] for h in range(fanout)]
    across_panel = lax.all_gather(
        turned_pieces, "row", axis=0, tiled=False, axis_index_groups=parts
    )

    factor, inverse = factor_and_inverse(0.5 * (corner + corner.T), block_size)
    weights = inverse.reshape(panel_width, panel_tiles, grid_cols, block_size)
    weights = weights.transpose(2, 1, 3, 0).reshape(grid_cols, piece_width, panel_width)

    own = jnp.einsum("crw,cwn->rn", own_panel, weights, precision=HIGHEST_PRECISION)
    own = own.reshape(tile_rows, block_size, panel_width)
    own_blocks = jnp.arange(tile_rows) * grid_rows + row_index
    own_below = (own_blocks >= PB)[:, None, None]
    top = lax.dynamic_slice_in_dim(
        factor, jnp.minimum(row_index, PB - 1) * block_size, block_size, axis=0
    )
    heads = jnp.where(own_below, own, top[None]).reshape(local_rows, panel_width)
    own_halves = split_halves(jnp.where(own_below, own, 0.0).reshape(local_rows, panel_width))
    weight_halves = split_halves(weights)
    in_top = (jnp.arange(fanout) * grid_cols + col_index < PB).astype(jnp.int32)
    across_halves = make_across(across_panel, weight_halves, in_top, tile_rows, diag_tiles)

    flat = front.reshape(tile_rows, block_size * tile_cols, block_size)
    base = make_base(
        flat, own_halves, across_halves, heads, early, row_table, early_table, place,
        panel_tiles, tile_cols,
    )
    result = make_final(base, late, row_table, late_table, tile_cols)
    return result.reshape(front.shape)


def solution(mesh):
    in_specs = (P(None, "row", None, "col"), P("row", "col"), P(), P())
    out_specs = P(None, "row", None, "col")
    return jax.shard_map(body, mesh=mesh, in_specs=in_specs, out_specs=out_specs, check_vma=False)
```
